32 devices in a mesh: section: 4 (over z), lon: 8 (over y, x, core).
Axes of the slice: x: 2, y: 2, z: 4, core: 2. Of those that a mesh axis runs over, the one named last changes fastest.
Arguments:
- lanczos_block: bfloat16 [16, 4, 64, 512], P(None, None, 'lon'), may hold values from -9 to 9
- previous: bfloat16 [16, 4, 64, 512], P(None, 'section', 'lon'), may hold values from -6 to 6
- beta_prev: float32 [16, 16], replicated, may hold values from -2 to 2, as said below
- weights: bfloat16 [4, 9, 512, 512], P('section'), may hold values from -0.09375 to 0.09375
- act_slope: bfloat16 [4, 4, 64, 512], P('section', None, 'lon'), may hold values from 0 to 1.09375
- metric: float32 [4, 64], P(None, 'lon'), may hold values from 0.3 to 3
Outputs:
- residual_block: float32 [16, 4, 64, 512], P(None, 'section', 'lon')
- projection: float32 [16, 16], replicated
- residual_gram: float32 [16, 16], replicated
The draws below stay inside these ranges and needn't reach their ends.
Inputs may be any that keep to these rules, and one draw needn't show every extreme that they name: `beta_prev`: upper triangular, with a positive diagonal.
All inputs are finite; a program needn't handle non-finite values.
Results may differ from the reference program's by a relative error of at most 0.02.
Values may be sent and summed in bfloat16 or wider, within the bound.
A program may use at most 64 MiB of HBM per device.

```python
import math
import jax
import jax.numpy as jnp
from jax import lax

C = 512
K = 16
DILATION_SIZE = 4
LAT = 4
LON = 64
LAYERS = 4


def draw_lanczos_block(key, part):
    lat_pos = jnp.arange(LAT, dtype=jnp.float32) / max(LAT - 1, 1)
    lon_pos = jnp.arange(LON, dtype=jnp.float32) / max(LON - 1, 1)
    amplitude = 0.5 * jnp.sqrt((1.0 + 2.0 * lat_pos)[:, None] * (1.0 + 2.0 * lon_pos)[None, :])
    base_values = jax.random.normal(key, (K, LAT, LON, C), jnp.float32)
    base_values = jnp.clip(base_values, -6.0, 6.0)
    return (base_values * amplitude[None, :, :, None]).astype(jnp.bfloat16)


def draw_beta_prev(key, part):
    first_key, second_key = jax.random.split(key)
    diagonal_part = jax.random.uniform(first_key, (K,), jnp.float32, 0.5, 1.5)
    upper_part = jnp.clip(0.3 * jax.random.normal(second_key, (K, K), jnp.float32), -1.5, 1.5)
    return jnp.triu(upper_part, 1) + jnp.diag(diagonal_part)


def steps_of(stream_key, shape, shards, least, largest):
    def one(axis_at, shards_of):
        draws = jax.random.uniform(jax.random.fold_in(jax.random.fold_in(stream_key, 6), axis_at), (shards_of,), jnp.float32, least / len(shards), largest / len(shards))
        return jnp.repeat(jnp.exp(draws), shape[axis_at] // shards_of).reshape((-1,) + (1,) * (len(shape) - axis_at - 1))

    loudness = one(*shards[0])
    for cut in shards[1:]:
        loudness = loudness * one(*cut)
    return loudness


def gaussian(rng, dims, spread, bound, cuts=(), held_as=jnp.bfloat16):
    array = spread * jax.random.normal(rng, dims, jnp.float32)
    if cuts:
        array = array * steps_of(rng, dims, cuts, -0.22, 0.18)
    return jnp.clip(array, -bound, bound).astype(held_as)


def setup_inputs(seed: int = 0) -> dict:
    keys = jax.random.split(jax.random.key(seed), 7)
    return {
        "lanczos_block": draw_lanczos_block(jax.random.fold_in(keys[6], 71), 0),
        "previous": gaussian(keys[1], (K, LAT, LON, C), 1.0, 6.0, ((1, 4), (2, 8))),
        "beta_prev": draw_beta_prev(jax.random.fold_in(keys[6], 71), 0),
        "weights": gaussian(keys[3], (LAYERS, 9, C, C), (9 * C) ** -0.5, 0.09375, ((0, 4),)),
        "act_slope": jnp.clip(1.09375 * jax.random.uniform(keys[4], (LAYERS, LAT, LON, C), jnp.float32) ** steps_of(keys[4], (LAYERS, LAT, LON, C), ((0, 4), (2, 8)), -0.2, 0.2), 0.0, 1.09375).astype(jnp.bfloat16),
        "metric": jnp.clip(jnp.exp(math.log(3.0) - 2.3025851 * jax.random.uniform(keys[5], (LAT, LON), jnp.float32) ** steps_of(keys[5], (LAT, LON), ((1, 8),), -0.2, 0.2)), 0.3, 3.0),
    }


def shifted_tap(input_field, row_stride, column_stride, direction_sign):
    rolled_field = jnp.roll(input_field, -direction_sign * column_stride * DILATION_SIZE, axis=2)
    padded_field = jnp.pad(rolled_field, ((0, 0), (DILATION_SIZE, DILATION_SIZE), (0, 0), (0, 0)))
    first_row = DILATION_SIZE + direction_sign * row_stride * DILATION_SIZE
    return padded_field[:, first_row:first_row + LAT]


def convolve(input_field, tap_weights, direction_sign):
    summed = jnp.zeros((input_field.shape[0] * LAT * LON, C), jnp.float32)
    for row_stride in (-1, 0, 1):
        for column_stride in (-1, 0, 1):
            tap_index = 3 * (row_stride + 1) + (column_stride + 1)
            tap_rows = shifted_tap(input_field, row_stride, column_stride, direction_sign).reshape(-1, C)
            tap_matrix = tap_weights[tap_index]
            if direction_sign < 0:
                tap_matrix = tap_matrix.T
            summed = summed + jnp.dot(tap_rows, tap_matrix, preferred_element_type=jnp.float32)
    return summed.reshape(input_field.shape)


def reference(lanczos_block, previous, beta_prev, weights, act_slope, metric):
    tangent = lanczos_block
    for layer_index in range(LAYERS):
        convolved = convolve(tangent, weights[layer_index], 1)
        slope_now = act_slope[layer_index].astype(jnp.float32)[None]
        tangent = (tangent.astype(jnp.float32) + slope_now * convolved).astype(jnp.bfloat16)
    cotangent = (metric[None, :, :, None] * tangent.astype(jnp.float32)).astype(jnp.bfloat16)
    for layer_index in range(LAYERS - 1, -1, -1):
        slope_now = act_slope[layer_index].astype(jnp.float32)[None]
        sensitivity = (slope_now * cotangent.astype(jnp.float32)).astype(jnp.bfloat16)
        convolved = convolve(sensitivity, weights[layer_index], -1)
        cotangent = (cotangent.astype(jnp.float32) + convolved).astype(jnp.bfloat16)
    cell_count = LAT * LON * C
    high = lax.Precision.HIGHEST
    block_flat = lanczos_block.reshape(K, -1).astype(jnp.float32)
    prev_flat = previous.reshape(K, -1).astype(jnp.float32)
    shifted = cotangent.reshape(K, -1).astype(jnp.float32) - jnp.dot(beta_prev, prev_flat, precision=high)
    projection = jnp.dot(block_flat, shifted.T, precision=high) / cell_count
    residual_rows = shifted - jnp.dot(projection.T, block_flat, precision=high)
    residual_gram = jnp.dot(residual_rows, residual_rows.T, precision=high) / cell_count
    return residual_rows.reshape(lanczos_block.shape), projection, residual_gram
```

```python
import functools

import jax
import jax.numpy as jnp
from jax import lax
from jax.experimental import pallas as pl
from jax.experimental.pallas import tpu as pltpu
from jax.sharding import PartitionSpec as P

K = 16
DILATION_SIZE = 4
LON_DEVICES = 8


def padded(cells, sides, width):
    for axis, dim in sides:
        count = lax.axis_size(axis)
        head = lax.slice_in_dim(cells, 0, width, axis=dim)
        tail = lax.slice_in_dim(cells, cells.shape[dim] - width, cells.shape[dim], axis=dim)
        cells = jnp.concatenate(
            [
                lax.ppermute(tail, axis, [(i, (i + 1) % count) for i in range(count)]),
                cells,
                lax.ppermute(head, axis, [((i + 1) % count, i) for i in range(count)]),
            ],
            axis=dim,
        )
    return cells


def from_behind(shard, axis, by):
    count = lax.axis_size(axis)
    pairs = [(i, i + by) for i in range(count) if 0 <= i + by < count]
    return lax.ppermute(shard, axis, pairs)


def broadcast(shard, axis, root):
    mine = lax.axis_index(axis) == root
    return lax.psum(jnp.where(mine, shard, jnp.zeros_like(shard)), axis)


def spread_taps(input_field, tap_weights, direction_sign, border_width):
    micro_size = input_field.shape[0]
    lat_rows = input_field.shape[1]
    lon_cols = input_field.shape[2] - 2 * border_width
    channels = input_field.shape[3]
    padded_field = jnp.pad(input_field, ((0, 0), (border_width, border_width), (0, 0), (0, 0)))
    summed = jnp.zeros((micro_size * lat_rows * lon_cols, channels), jnp.float32)
    for row_stride in (-1, 0, 1):
        for column_stride in (-1, 0, 1):
            tap_index = 3 * (row_stride + 1) + (column_stride + 1)
            first_row = border_width + direction_sign * row_stride * border_width
            col_start = border_width + direction_sign * column_stride * border_width
            tap_rows = padded_field[
                :, first_row : first_row + lat_rows, col_start : col_start + lon_cols, :
            ].reshape(-1, channels)
            if direction_sign > 0:
                summed = summed + jnp.dot(
                    tap_rows, tap_weights[tap_index], preferred_element_type=jnp.float32
                )
            else:
                summed = summed + lax.dot_general(
                    tap_rows,
                    tap_weights[tap_index],
                    (((1,), (1,)), ((), ())),
                    preferred_element_type=jnp.float32,
                )
    return summed.reshape(micro_size, lat_rows, lon_cols, channels)


def body(lanczos_block, previous, beta_prev, weights, act_slope, metric):
    section_count = lax.axis_size("section")
    section_index = lax.axis_index("section")
    tap_weights = weights[0]
    slope_here = act_slope[0].astype(jnp.float32)[None]
    border_width = DILATION_SIZE
    micro_count = 2
    micro_size = K // micro_count
    slot_shape = (micro_size,) + lanczos_block.shape[1:]
    lon_cols = lanczos_block.shape[2]
    micro_feeds = lanczos_block.reshape((micro_count,) + slot_shape)
    tick_count = micro_count + section_count - 1
    zero_slot = jnp.zeros(slot_shape, jnp.bfloat16)
    empty_store = jnp.zeros((micro_count,) + slot_shape, jnp.bfloat16)

    def forward_layer(rimmed):
        convolved = spread_taps(rimmed, tap_weights, 1, border_width)
        centre = rimmed[:, :, border_width : border_width + lon_cols, :].astype(jnp.float32)
        return (centre + slope_here * convolved).astype(jnp.bfloat16)

    def skip_forward(rimmed):
        return zero_slot

    def forward_tick(state_pair, tick_now):
        inbound, forward_out = state_pair
        micro_index = tick_now - section_index
        active = (micro_index >= 0) & (micro_index < micro_count)
        slot_index = jnp.clip(micro_index, 0, micro_count - 1)
        fed_slot = lax.dynamic_index_in_dim(micro_feeds, slot_index, 0, keepdims=False)
        incoming = jnp.where(section_index == 0, fed_slot, inbound)
        rimmed = padded(incoming, (("lon", 2),), border_width)
        result = lax.cond(active, forward_layer, skip_forward, rimmed)
        keep_slot = active & (section_index == section_count - 1)
        old_slot = lax.dynamic_index_in_dim(forward_out, slot_index, 0, keepdims=False)
        forward_out = lax.dynamic_update_index_in_dim(
            forward_out, jnp.where(keep_slot, result, old_slot), slot_index, 0
        )
        outbound = from_behind(result, "section", 1)
        return ((outbound, forward_out), None)

    (unused_slot, forward_out), unused_out = lax.scan(
        forward_tick, (zero_slot, empty_store), jnp.arange(tick_count, dtype=jnp.int32)
    )
    metric_here = metric[None, :, :, None]

    def backward_layer(operands):
        incoming, rimmed = operands
        convolved = spread_taps(rimmed, tap_weights, -1, border_width)
        return (incoming.astype(jnp.float32) + convolved).astype(jnp.bfloat16)

    def skip_backward(operands):
        return zero_slot

    def backward_tick(state_pair, tick_now):
        inbound, adjoint_out = state_pair
        micro_index = tick_now - (section_count - 1 - section_index)
        active = (micro_index >= 0) & (micro_index < micro_count)
        slot_index = jnp.clip(micro_index, 0, micro_count - 1)
        stored_slot = lax.dynamic_index_in_dim(forward_out, slot_index, 0, keepdims=False)
        started = (metric_here * stored_slot.astype(jnp.float32)).astype(jnp.bfloat16)
        incoming = jnp.where(section_index == section_count - 1, started, inbound)
        sensitivity = (slope_here * incoming.astype(jnp.float32)).astype(jnp.bfloat16)
        rimmed = padded(sensitivity, (("lon", 2),), border_width)
        result = lax.cond(active, backward_layer, skip_backward, (incoming, rimmed))
        keep_slot = active & (section_index == 0)
        old_slot = lax.dynamic_index_in_dim(adjoint_out, slot_index, 0, keepdims=False)
        adjoint_out = lax.dynamic_update_index_in_dim(
            adjoint_out, jnp.where(keep_slot, result, old_slot), slot_index, 0
        )
        outbound = from_behind(result, "section", -1)
        return ((outbound, adjoint_out), None)

    (unused_back, adjoint_out), unused_more = lax.scan(
        backward_tick, (zero_slot, empty_store), jnp.arange(tick_count, dtype=jnp.int32)
    )
    applied = adjoint_out.reshape(lanczos_block.shape)
    applied_all = broadcast(applied, "section", 0)
    row_count = previous.shape[1]
    applied_rows = lax.dynamic_slice_in_dim(applied_all, section_index * row_count, row_count, 1)
    own_block = lax.dynamic_slice_in_dim(lanczos_block, section_index * row_count, row_count, 1)
    high = lax.Precision.HIGHEST
    cell_count = (
        lanczos_block.shape[1]
        * lanczos_block.shape[2]
        * lax.axis_size("lon")
        * lanczos_block.shape[3]
    )
    block_flat = own_block.reshape(K, -1).astype(jnp.float32)
    prev_flat = previous.reshape(K, -1).astype(jnp.float32)
    shifted = applied_rows.reshape(K, -1).astype(jnp.float32) - jnp.dot(
        beta_prev, prev_flat, precision=high
    )
    part_projection = jnp.dot(block_flat, shifted.T, precision=high) / cell_count
    part_shifted = jnp.dot(shifted, shifted.T, precision=high) / cell_count
    part_block = jnp.dot(block_flat, block_flat.T, precision=high) / cell_count
    projection, shifted_gram, block_gram = lax.psum(
        (part_projection, part_shifted, part_block), ("section", "lon")
    )
    residual_rows = shifted - jnp.dot(projection.T, block_flat, precision=high)
    squared_proj = jnp.dot(projection.T, projection, precision=high)
    weighted = jnp.dot(
        projection.T, jnp.dot(block_gram, projection, precision=high), precision=high
    )
    residual_gram = shifted_gram - 2.0 * squared_proj + weighted
    return (residual_rows.reshape(own_block.shape), projection, residual_gram)


def ring_kernel(
    sections, band, cells, block_ref, prev_ref, beta_ref, weights_ref, slope_ref, metric_ref,
    resid_ref, proj_ref, gram_ref,
    taps_held, block_rows, block_in, slope_own, slope_z, slope_all, slope_wide, metric_all,
    field, applied_out, applied_in, part_a, part_b,
    own_sem, zs_send, zs_recv, zw_send, zw_recv, sl_send, sl_recv, me_send, me_recv,
    st_send, st_recv, in_send, in_recv, out_send, out_recv, pa_send, pa_recv, pb_send, pb_recv,
):
    f32, bf16 = jnp.float32, jnp.bfloat16
    high = lax.Precision.HIGHEST
    s = lax.axis_index("section")
    l = lax.axis_index("lon")
    lons = LON_DEVICES
    taps = 3
    channels = block_ref.shape[3]
    pairs = block_ref.shape[0] // lons
    rows = lons * pairs * band
    slab = pairs * band
    half = band // 2
    layers = sections

    core = lax.rem(l, 2)
    xbit = lax.rem(l // 2, 2)
    ybit = l // 4
    flip_x = l + 2 - 4 * xbit
    flip_y = l + 4 - 8 * ybit
    flip_core = l + 1 - 2 * core
    first = flip_x * (1 - core) + flip_y * core
    second = flip_y * (1 - core) + flip_x * core
    abit = xbit * (1 - core) + ybit * core
    bbit = ybit * (1 - core) + xbit * core
    place = 4 * core + 2 * bbit + abit
    partners = (first, second, flip_core)

    def place_of(device):
        c, x, y = device % 2, (device // 2) % 2, device // 4
        return 4 * c + (2 * y + x if c == 0 else 2 * x + y)

    def remote(src, dst, send, recv, section, lon):
        return pltpu.make_async_remote_copy(
            src_ref=src, dst_ref=dst, send_sem=send, recv_sem=recv,
            device_id=(section, lon), device_id_type=pl.DeviceIdType.MESH,
        )

    def other(i):
        return i + (i - s + layers) // layers

    own_copy = pltpu.make_async_copy(weights_ref.at[0, pl.ds(taps, taps)], taps_held.at[s], own_sem)
    own_copy.start()

    barrier = pltpu.get_barrier_semaphore()
    for d in range(1, sections):
        pl.semaphore_signal(
            barrier, inc=1, device_id=(lax.rem(s + d, sections), l),
            device_id_type=pl.DeviceIdType.MESH,
        )
    for d in range(1, lons):
        pl.semaphore_signal(
            barrier, inc=1, device_id=(s, lax.rem(l + d, lons)),
            device_id_type=pl.DeviceIdType.MESH,
        )

    slope_own[...] = slope_ref[0].astype(f32)
    slope_z[s] = slope_own[s]
    block_f = block_ref[:, s].astype(f32).reshape(rows, channels)
    block_rows[...] = block_f.astype(bf16).reshape(lons, slab, channels)
    block_in[l] = block_rows[l]
    metric_row = metric_ref[pl.ds(s, 1), :]
    eye = lax.broadcasted_iota(jnp.int32, (band, band), 0) == lax.broadcasted_iota(
        jnp.int32, (band, band), 1
    )
    metric_col = jnp.sum(
        jnp.where(eye, jnp.broadcast_to(metric_row, (band, band)), 0.0), axis=1, keepdims=True
    )
    metric_all[place] = jnp.broadcast_to(metric_col, (band, 128))

    pl.semaphore_wait(barrier, sections - 1 + lons - 1)

    sends = []

    def launch(copy):
        copy.start()
        sends.append(copy)

    chunk = channels // lons
    for d in range(1, sections):
        to = lax.rem(s + d, sections)
        launch(remote(slope_own.at[to], slope_z.at[s], zs_send.at[d], zs_recv.at[s], to, l))
    mine = pl.ds(pl.multiple_of(place * chunk, chunk), chunk)
    for t in range(taps):
        for d in range(1, sections):
            to = lax.rem(s + d, sections)
            launch(remote(
                weights_ref.at[0, taps + t, mine], taps_held.at[s, t, mine],
                zw_send.at[d, t], zw_recv.at[s, t], to, l,
            ))
    for d in range(1, lons):
        to = lax.rem(l + d, lons)
        launch(remote(block_rows.at[to], block_in.at[l], in_send.at[d], in_recv.at[l], s, to))

    spans = (
        (place, 1),
        (2 * (place // 2), 2),
        (4 * core, 4),
    )
    arrive = (
        (place + 1 - 2 * abit, 1),
        (2 * (place // 2) + 2 - 4 * bbit, 2),
        (4 - 4 * core, 4),
    )

    def slope_copies(stage, where):
        at, size = where[stage]
        span = pl.ds(at, size)
        return (
            remote(slope_all.at[span], slope_all.at[span], sl_send.at[stage], sl_recv.at[stage],
                   s, partners[stage]),
            remote(metric_all.at[span], metric_all.at[span], me_send.at[stage], me_recv.at[stage],
                   s, partners[stage]),
        )

    def weight_copy(stage, unit, where):
        at, size = where[stage]
        span = pl.ds(pl.multiple_of(at * chunk, chunk), size * chunk)
        held = taps_held.at[other(unit // taps), unit % taps, span]
        return remote(held, held, st_send.at[stage, unit], st_recv.at[stage, unit], s, partners[stage])

    def advance(step):
        units = (sections - 1) * taps
        for stage in range(3):
            unit = step - stage
            if 0 <= unit <= units:
                if unit == 0:
                    if stage == 0:
                        for i in range(sections - 1):
                            ly = other(i)
                            remote(slope_own.at[0], slope_z.at[ly], zs_send.at[0], zs_recv.at[ly],
                                   s, l).wait_recv()
                        slope_all[place] = slope_z[...].reshape(layers * band, channels).astype(bf16)
                    else:
                        for copy in slope_copies(stage - 1, arrive):
                            copy.wait_recv()
                    for copy in slope_copies(stage, spans):
                        launch(copy)
                else:
                    u = unit - 1
                    if stage == 0:
                        held = taps_held.at[other(u // taps), u % taps, mine]
                        remote(held, held, zw_send.at[0, 0], zw_recv.at[other(u // taps), u % taps],
                               s, l).wait_recv()
                    else:
                        weight_copy(stage - 1, u, arrive).wait_recv()
                    launch(weight_copy(stage, u, spans))
        unit = step - 3
        if unit == 0:
            for copy in slope_copies(2, arrive):
                copy.wait_recv()
        elif 0 < unit <= units:
            weight_copy(2, unit - 1, arrive).wait_recv()

    def widen():
        for b in range(lons):
            slope_wide[:, b] = slope_all[place_of(b)].astype(f32).reshape(layers, band, channels)

    low = lax.broadcasted_iota(jnp.int32, (lons, pairs, band, channels), 2) < half

    def neighbours(values):
        swapped = pltpu.roll(values.reshape(lons * pairs, band, channels), half, 1)
        swapped = swapped.reshape(lons, pairs, band, channels)
        after = jnp.concatenate([swapped[1:], swapped[:1]], axis=0)
        before = jnp.concatenate([swapped[-1:], swapped[:-1]], axis=0)
        plus = jnp.where(low, swapped, after)
        minus = jnp.where(low, before, swapped)
        return (minus.reshape(rows, channels).astype(bf16), plus.reshape(rows, channels).astype(bf16))

    def forward(n):
        u = field[...].astype(f32)
        minus, plus = neighbours(u)
        conv = jnp.dot(minus, taps_held[n, 0], preferred_element_type=f32)
        conv = conv + jnp.dot(u.astype(bf16), taps_held[n, 1], preferred_element_type=f32)
        conv = conv + jnp.dot(plus, taps_held[n, 2], preferred_element_type=f32)
        slope = slope_wide[n][:, None]
        out = u.reshape(lons, pairs, band, channels) + slope * conv.reshape(lons, pairs, band, channels)
        field[...] = out.reshape(rows, channels).astype(bf16)

    def backward(n):
        c = field[...].astype(f32)
        slope = slope_wide[n][:, None]
        sens = (slope * c.reshape(lons, pairs, band, channels)).reshape(rows, channels).astype(bf16)
        minus, plus = neighbours(sens.astype(f32))
        flip = (((1,), (1,)), ((), ()))
        conv = lax.dot_general(plus, taps_held[n, 0], flip, preferred_element_type=f32)
        conv = conv + lax.dot_general(sens, taps_held[n, 1], flip, preferred_element_type=f32)
        conv = conv + lax.dot_general(minus, taps_held[n, 2], flip, preferred_element_type=f32)
        field[...] = (c + conv).astype(bf16)

    for step in range(3):
        advance(step)

    count = lons * pairs
    row_id = lax.broadcasted_iota(jnp.int32, (rows, 128), 0)
    col_id = lax.broadcasted_iota(jnp.int32, (rows, 128), 1)
    vec_of = row_id // band
    onto = [jnp.where(col_id == count * i + vec_of, 1.0, 0.0).astype(f32) for i in range(3)]
    fold = jnp.where(
        lax.broadcasted_iota(jnp.int32, (count, rows), 0)
        == lax.broadcasted_iota(jnp.int32, (count, rows), 1) // band, 1.0, 0.0
    ).astype(f32)
    expand = onto[0][:, :count]
    same = lax.rem(lax.broadcasted_iota(jnp.int32, (rows, rows), 0), band) == lax.rem(
        lax.broadcasted_iota(jnp.int32, (rows, rows), 1), band
    )
    nt = (((1,), (1,)), ((), ()))

    def dot(a, b):
        return jnp.dot(a, b, precision=high, preferred_element_type=f32)

    def dot_nt(a, b):
        return lax.dot_general(a, b, nt, precision=high, preferred_element_type=f32)

    beta_wide = jnp.where(same, dot_nt(dot(expand, beta_ref[...]), expand), 0.0)
    prev_f = prev_ref[:, 0].astype(f32).reshape(rows, channels)
    resid_ref[...] = dot(beta_wide, prev_f)
    own_bf = block_rows[...].reshape(rows, channels)
    gram_b = lax.dot_general(own_bf, own_bf, nt, preferred_element_type=f32)
    part_b_early = dot(jnp.where(same, gram_b, 0.0), onto[2])

    advance(3)
    widen()
    for d in range(1, lons):
        source = lax.rem(l + d, lons)
        remote(block_rows.at[0], block_in.at[source], in_send.at[0], in_recv.at[source],
               s, l).wait_recv()
    field[...] = block_in[...].reshape(rows, channels)
    own_copy.wait()

    for n in range(sections - 1):
        for t in range(taps):
            advance(4 + n * taps + t)
        forward(n)
    forward(sections - 1)
    t4 = field[...].astype(f32).reshape(lons, pairs, band, channels)
    for b in range(lons):
        scale = metric_all[place_of(b)][:, :1]
        field[pl.ds(b * slab, slab)] = (scale[None] * t4[b]).reshape(slab, channels).astype(bf16)
    for n in range(sections - 1, -1, -1):
        backward(n)

    applied_out[...] = field[...].reshape(lons, slab, channels)
    for d in range(1, lons):
        to = lax.rem(l + d, lons)
        launch(remote(applied_out.at[to], applied_in.at[l], out_send.at[d], out_recv.at[l], s, to))
    applied_in[l] = applied_out[l]
    for d in range(1, lons):
        source = lax.rem(l + d, lons)
        remote(applied_out.at[0], applied_in.at[source], out_send.at[0], out_recv.at[source],
               s, l).wait_recv()
    shifted = applied_in[...].reshape(rows, channels).astype(f32) - resid_ref[...]
    own_f = own_bf.astype(f32)
    gram_p = jnp.where(same, dot_nt(own_f, shifted), 0.0)
    gram_s = jnp.where(same, dot_nt(shifted, shifted), 0.0)
    part = dot(fold, dot(gram_p, onto[0]) + dot(gram_s, onto[1]) + part_b_early)

    part_a[l] = part
    for d in range(1, lons):
        to = lax.rem(l + d, lons)
        launch(remote(part_a.at[l], part_a.at[l], pa_send.at[d], pa_recv.at[l], s, to))
    for d in range(1, lons):
        source = lax.rem(l + d, lons)
        remote(part_a.at[source], part_a.at[source], pa_send.at[0], pa_recv.at[source],
               s, l).wait_recv()
    part_b[s] = jnp.sum(part_a[...], axis=0)
    for d in range(1, sections):
        to = lax.rem(s + d, sections)
        launch(remote(part_b.at[s], part_b.at[s], pb_send.at[d], pb_recv.at[s], to, l))
    for d in range(1, sections):
        source = lax.rem(s + d, sections)
        remote(part_b.at[source], part_b.at[source], pb_send.at[0], pb_recv.at[source],
               s, l).wait_recv()
    total = jnp.sum(part_b[...], axis=0) / cells
    projection = total[:, :count]
    shifted_gram = total[:, count : 2 * count]
    block_gram = total[:, 2 * count : 3 * count]
    proj_ref[...] = projection
    tn = (((0,), (0,)), ((), ()))
    bp = dot(block_gram, projection)
    inner = lax.dot_general(
        projection, bp - 2.0 * projection, tn, precision=high, preferred_element_type=f32
    )
    gram_ref[...] = shifted_gram + inner
    proj_wide = jnp.where(same, dot_nt(dot_nt(expand, projection), expand), 0.0)
    resid_ref[...] = shifted - dot(proj_wide, own_f)
    for copy in sends:
        copy.wait_send()


def ring_body(lanczos_block, previous, beta_prev, weights, act_slope, metric):
    f32, bf16 = jnp.float32, jnp.bfloat16
    sections = lax.axis_size("section")
    lons = lax.axis_size("lon")
    count, lat, band, channels = lanczos_block.shape
    pairs = count // lons
    rows = count * band
    slab = pairs * band
    taps = 3
    cells = lat * band * lons * channels
    vmem = pl.BlockSpec(memory_space=pltpu.VMEM)
    dma = pltpu.SemaphoreType.DMA
    units = (sections - 1) * taps
    resid, proj, gram = pl.pallas_call(
        functools.partial(ring_kernel, sections, band, float(cells)),
        out_shape=(
            jax.ShapeDtypeStruct((rows, channels), f32),
            jax.ShapeDtypeStruct((count, count), f32),
            jax.ShapeDtypeStruct((count, count), f32),
        ),
        in_specs=[vmem, vmem, vmem, pl.BlockSpec(memory_space=pl.ANY), vmem, vmem],
        out_specs=(vmem, vmem, vmem),
        scratch_shapes=[
            pltpu.VMEM((sections, taps, channels, channels), bf16),
            pltpu.VMEM((lons, slab, channels), bf16),
            pltpu.VMEM((lons, slab, channels), bf16),
            pltpu.VMEM((lat, band, channels), f32),
            pltpu.VMEM((sections, band, channels), f32),
            pltpu.VMEM((lons, sections * band, channels), bf16),
            pltpu.VMEM((sections, lons, band, channels), f32),
            pltpu.VMEM((lons, band, 128), f32),
            pltpu.VMEM((rows, channels), bf16),
            pltpu.VMEM((lons, slab, channels), bf16),
            pltpu.VMEM((lons, slab, channels), bf16),
            pltpu.VMEM((lons, count, 128), f32),
            pltpu.VMEM((sections, count, 128), f32),
            dma,
            dma((sections,)), dma((sections,)),
            dma((sections, taps)), dma((sections, taps)),
            dma((3,)), dma((3,)), dma((3,)), dma((3,)),
            dma((3, units)), dma((3, units)),
            dma((lons,)), dma((lons,)), dma((lons,)), dma((lons,)),
            dma((lons,)), dma((lons,)), dma((sections,)), dma((sections,)),
        ],
        compiler_params=pltpu.CompilerParams(
            collective_id=0, has_side_effects=True, vmem_limit_bytes=48 * 1024 * 1024
        ),
    )(lanczos_block, previous, beta_prev, weights, act_slope, metric)
    return (resid.reshape(count, previous.shape[1], band, channels), proj, gram)


def step_body(lanczos_block, previous, beta_prev, weights, act_slope, metric):
    count, lat, band, channels = lanczos_block.shape
    lons = lax.axis_size("lon")
    sections = lax.axis_size("section")
    rings = (
        lat <= DILATION_SIZE
        and lat == sections
        and lons == LON_DEVICES
        and band == 2 * DILATION_SIZE
        and count % lons == 0
        and (count // lons * band) % 16 == 0
        and 3 * count <= 128
        and channels % (16 * lons) == 0
    )
    form = ring_body if rings else body
    return form(lanczos_block, previous, beta_prev, weights, act_slope, metric)


def solution(mesh):
    return jax.shard_map(
        step_body,
        mesh=mesh,
        in_specs=(
            P(None, None, "lon", None),
            P(None, "section", "lon", None),
            P(),
            P("section", None, None, None),
            P("section", None, "lon", None),
            P(None, "lon"),
        ),
        out_specs=(P(None, "section", "lon", None), P(), P()),
        check_vma=False,
    )
```

```python
import functools

import jax
import jax.numpy as jnp
from jax import lax
from jax.experimental import pallas as pl
from jax.experimental.pallas import tpu as pltpu
from jax.sharding import PartitionSpec as P

K = 16
DILATION_SIZE = 4
LON_DEVICES = 8
SKEW = 3


def padded(cells, sides, width):
    for axis, dim in sides:
        count = lax.axis_size(axis)
        head = lax.slice_in_dim(cells, 0, width, axis=dim)
        tail = lax.slice_in_dim(cells, cells.shape[dim] - width, cells.shape[dim], axis=dim)
        cells = jnp.concatenate(
            [
                lax.ppermute(tail, axis, [(i, (i + 1) % count) for i in range(count)]),
                cells,
                lax.ppermute(head, axis, [((i + 1) % count, i) for i in range(count)]),
            ],
            axis=dim,
        )
    return cells


def from_behind(shard, axis, by):
    count = lax.axis_size(axis)
    pairs = [(i, i + by) for i in range(count) if 0 <= i + by < count]
    return lax.ppermute(shard, axis, pairs)


def broadcast(shard, axis, root):
    mine = lax.axis_index(axis) == root
    return lax.psum(jnp.where(mine, shard, jnp.zeros_like(shard)), axis)


def spread_taps(input_field, tap_weights, direction_sign, border_width):
    micro_size = input_field.shape[0]
    lat_rows = input_field.shape[1]
    lon_cols = input_field.shape[2] - 2 * border_width
    channels = input_field.shape[3]
    padded_field = jnp.pad(input_field, ((0, 0), (border_width, border_width), (0, 0), (0, 0)))
    summed = jnp.zeros((micro_size * lat_rows * lon_cols, channels), jnp.float32)
    for row_stride in (-1, 0, 1):
        for column_stride in (-1, 0, 1):
            tap_index = 3 * (row_stride + 1) + (column_stride + 1)
            first_row = border_width + direction_sign * row_stride * border_width
            col_start = border_width + direction_sign * column_stride * border_width
            tap_rows = padded_field[
                :, first_row : first_row + lat_rows, col_start : col_start + lon_cols, :
            ].reshape(-1, channels)
            if direction_sign > 0:
                summed = summed + jnp.dot(
                    tap_rows, tap_weights[tap_index], preferred_element_type=jnp.float32
                )
            else:
                summed = summed + lax.dot_general(
                    tap_rows,
                    tap_weights[tap_index],
                    (((1,), (1,)), ((), ())),
                    preferred_element_type=jnp.float32,
                )
    return summed.reshape(micro_size, lat_rows, lon_cols, channels)


def body(lanczos_block, previous, beta_prev, weights, act_slope, metric):
    section_count = lax.axis_size("section")
    section_index = lax.axis_index("section")
    tap_weights = weights[0]
    slope_here = act_slope[0].astype(jnp.float32)[None]
    border_width = DILATION_SIZE
    micro_count = 2
    micro_size = K // micro_count
    slot_shape = (micro_size,) + lanczos_block.shape[1:]
    lon_cols = lanczos_block.shape[2]
    micro_feeds = lanczos_block.reshape((micro_count,) + slot_shape)
    tick_count = micro_count + section_count - 1
    zero_slot = jnp.zeros(slot_shape, jnp.bfloat16)
    empty_store = jnp.zeros((micro_count,) + slot_shape, jnp.bfloat16)

    def forward_layer(rimmed):
        convolved = spread_taps(rimmed, tap_weights, 1, border_width)
        centre = rimmed[:, :, border_width : border_width + lon_cols, :].astype(jnp.float32)
        return (centre + slope_here * convolved).astype(jnp.bfloat16)

    def skip_forward(rimmed):
        return zero_slot

    def forward_tick(state_pair, tick_now):
        inbound, forward_out = state_pair
        micro_index = tick_now - section_index
        active = (micro_index >= 0) & (micro_index < micro_count)
        slot_index = jnp.clip(micro_index, 0, micro_count - 1)
        fed_slot = lax.dynamic_index_in_dim(micro_feeds, slot_index, 0, keepdims=False)
        incoming = jnp.where(section_index == 0, fed_slot, inbound)
        rimmed = padded(incoming, (("lon", 2),), border_width)
        result = lax.cond(active, forward_layer, skip_forward, rimmed)
        keep_slot = active & (section_index == section_count - 1)
        old_slot = lax.dynamic_index_in_dim(forward_out, slot_index, 0, keepdims=False)
        forward_out = lax.dynamic_update_index_in_dim(
            forward_out, jnp.where(keep_slot, result, old_slot), slot_index, 0
        )
        outbound = from_behind(result, "section", 1)
        return ((outbound, forward_out), None)

    (unused_slot, forward_out), unused_out = lax.scan(
        forward_tick, (zero_slot, empty_store), jnp.arange(tick_count, dtype=jnp.int32)
    )
    metric_here = metric[None, :, :, None]

    def backward_layer(operands):
        incoming, rimmed = operands
        convolved = spread_taps(rimmed, tap_weights, -1, border_width)
        return (incoming.astype(jnp.float32) + convolved).astype(jnp.bfloat16)

    def skip_backward(operands):
        return zero_slot

    def backward_tick(state_pair, tick_now):
        inbound, adjoint_out = state_pair
        micro_index = tick_now - (section_count - 1 - section_index)
        active = (micro_index >= 0) & (micro_index < micro_count)
        slot_index = jnp.clip(micro_index, 0, micro_count - 1)
        stored_slot = lax.dynamic_index_in_dim(forward_out, slot_index, 0, keepdims=False)
        started = (metric_here * stored_slot.astype(jnp.float32)).astype(jnp.bfloat16)
        incoming = jnp.where(section_index == section_count - 1, started, inbound)
        sensitivity = (slope_here * incoming.astype(jnp.float32)).astype(jnp.bfloat16)
        rimmed = padded(sensitivity, (("lon", 2),), border_width)
        result = lax.cond(active, backward_layer, skip_backward, (incoming, rimmed))
        keep_slot = active & (section_index == 0)
        old_slot = lax.dynamic_index_in_dim(adjoint_out, slot_index, 0, keepdims=False)
        adjoint_out = lax.dynamic_update_index_in_dim(
            adjoint_out, jnp.where(keep_slot, result, old_slot), slot_index, 0
        )
        outbound = from_behind(result, "section", -1)
        return ((outbound, adjoint_out), None)

    (unused_back, adjoint_out), unused_more = lax.scan(
        backward_tick, (zero_slot, empty_store), jnp.arange(tick_count, dtype=jnp.int32)
    )
    applied = adjoint_out.reshape(lanczos_block.shape)
    applied_all = broadcast(applied, "section", 0)
    row_count = previous.shape[1]
    applied_rows = lax.dynamic_slice_in_dim(applied_all, section_index * row_count, row_count, 1)
    own_block = lax.dynamic_slice_in_dim(lanczos_block, section_index * row_count, row_count, 1)
    high = lax.Precision.HIGHEST
    cell_count = (
        lanczos_block.shape[1]
        * lanczos_block.shape[2]
        * lax.axis_size("lon")
        * lanczos_block.shape[3]
    )
    block_flat = own_block.reshape(K, -1).astype(jnp.float32)
    prev_flat = previous.reshape(K, -1).astype(jnp.float32)
    shifted = applied_rows.reshape(K, -1).astype(jnp.float32) - jnp.dot(
        beta_prev, prev_flat, precision=high
    )
    part_projection = jnp.dot(block_flat, shifted.T, precision=high) / cell_count
    part_shifted = jnp.dot(shifted, shifted.T, precision=high) / cell_count
    part_block = jnp.dot(block_flat, block_flat.T, precision=high) / cell_count
    projection, shifted_gram, block_gram = lax.psum(
        (part_projection, part_shifted, part_block), ("section", "lon")
    )
    residual_rows = shifted - jnp.dot(projection.T, block_flat, precision=high)
    squared_proj = jnp.dot(projection.T, projection, precision=high)
    weighted = jnp.dot(
        projection.T, jnp.dot(block_gram, projection, precision=high), precision=high
    )
    residual_gram = shifted_gram - 2.0 * squared_proj + weighted
    return (residual_rows.reshape(own_block.shape), projection, residual_gram)


def ring_kernel(
    sections, band, cells, block_hbm, prev_hbm, beta_hbm, weights_ref, slope_hbm, metric_hbm,
    resid_ref, proj_ref, gram_ref,
    taps_held, block_rows, block_in, slope_own, slope_z, slope_all, slope_wide, metric_all,
    field, applied_out, applied_in, part_a, part_b,
    block_ref, prev_ref, beta_ref, slope_ref, metric_ref, load_sem,
    own_sem, zs_send, zs_recv, zw_send, zw_recv, sl_send, sl_recv, me_send, me_recv,
    st_send, st_recv, in_send, in_recv, out_send, out_recv, pa_send, pa_recv, pb_send, pb_recv,
):
    f32, bf16 = jnp.float32, jnp.bfloat16
    high = lax.Precision.HIGHEST
    s = lax.axis_index("section")
    l = lax.axis_index("lon")
    lons = LON_DEVICES
    taps = 3
    channels = block_hbm.shape[3]
    pairs = block_hbm.shape[0] // lons
    rows = lons * pairs * band
    slab = pairs * band
    half = band // 2
    layers = sections
    others = sections - 1

    core = lax.rem(l, 2)
    xbit = lax.rem(l // 2, 2)
    ybit = l // 4
    flip_x = l + 2 - 4 * xbit
    flip_y = l + 4 - 8 * ybit
    flip_core = l + 1 - 2 * core
    first = flip_x * (1 - core) + flip_y * core
    second = flip_y * (1 - core) + flip_x * core
    abit = xbit * (1 - core) + ybit * core
    bbit = ybit * (1 - core) + xbit * core
    place = 4 * core + 2 * bbit + abit
    partners = (first, second, flip_core)

    def place_of(device):
        c, x, y = device % 2, (device // 2) % 2, device // 4
        return 4 * c + (2 * y + x if c == 0 else 2 * x + y)

    def remote(src, dst, send, recv, section, lon):
        return pltpu.make_async_remote_copy(
            src_ref=src, dst_ref=dst, send_sem=send, recv_sem=recv,
            device_id=(section, lon), device_id_type=pl.DeviceIdType.MESH,
        )

    def other(i):
        return i + (i - s + layers) // layers

    loads = [
        pltpu.make_async_copy(source, held, load_sem.at[i])
        for i, (source, held) in enumerate((
            (slope_hbm, slope_ref),
            (metric_hbm, metric_ref),
            (block_hbm.at[:, s], block_ref),
            (prev_hbm, prev_ref),
            (beta_hbm, beta_ref),
        ))
    ]
    for load in loads:
        load.start()
    own_copy = pltpu.make_async_copy(weights_ref.at[0, pl.ds(taps, taps)], taps_held.at[s], own_sem)
    own_copy.start()

    barrier = pltpu.get_barrier_semaphore()
    for d in range(1, sections):
        pl.semaphore_signal(
            barrier, inc=1, device_id=(lax.rem(s + d, sections), l),
            device_id_type=pl.DeviceIdType.MESH,
        )
    for d in range(1, lons):
        pl.semaphore_signal(
            barrier, inc=1, device_id=(s, lax.rem(l + d, lons)),
            device_id_type=pl.DeviceIdType.MESH,
        )

    for load in loads[:3]:
        load.wait()
    slope_own[...] = slope_ref[0].astype(f32)
    slope_z[s] = slope_own[s]
    block_f = block_ref[...].astype(f32).reshape(rows, channels)
    block_rows[...] = block_f.astype(bf16).reshape(lons, slab, channels)
    block_in[l] = block_rows[l]
    metric_row = metric_ref[pl.ds(s, 1), :]
    eye = lax.broadcasted_iota(jnp.int32, (band, band), 0) == lax.broadcasted_iota(
        jnp.int32, (band, band), 1
    )
    metric_col = jnp.sum(
        jnp.where(eye, jnp.broadcast_to(metric_row, (band, band)), 0.0), axis=1, keepdims=True
    )
    metric_all[place] = jnp.broadcast_to(metric_col, (band, 128))

    pl.semaphore_wait(barrier, sections - 1 + lons - 1)

    sends = []

    def launch(copy):
        copy.start()
        sends.append(copy)

    chunk = channels // lons
    for d in range(1, sections):
        to = lax.rem(s + d, sections)
        launch(remote(slope_own.at[to], slope_z.at[s], zs_send.at[d], zs_recv.at[s], to, l))
    mine = pl.ds(pl.multiple_of(place * chunk, chunk), chunk)
    for t in range(taps):
        for d in range(1, sections):
            to = lax.rem(s + d, sections)
            launch(remote(
                weights_ref.at[0, taps + t, mine], taps_held.at[s, t, mine],
                zw_send.at[d, t], zw_recv.at[s, t], to, l,
            ))
    for d in range(1, lons):
        to = lax.rem(l + d, lons)
        launch(remote(block_rows.at[to], block_in.at[l], in_send.at[d], in_recv.at[l], s, to))

    spans = (
        (place, 1),
        (2 * (place // 2), 2),
        (4 * core, 4),
    )
    arrive = (
        (place + 1 - 2 * abit, 1),
        (2 * (place // 2) + 2 - 4 * bbit, 2),
        (4 - 4 * core, 4),
    )

    def slope_copies(stage, where):
        at, size = where[stage]
        span = pl.ds(at, size)
        return (
            remote(slope_all.at[span], slope_all.at[span], sl_send.at[stage], sl_recv.at[stage],
                   s, partners[stage]),
            remote(metric_all.at[span], metric_all.at[span], me_send.at[stage], me_recv.at[stage],
                   s, partners[stage]),
        )

    def weight_copy(stage, unit, where):
        at, size = where[stage]
        span = pl.ds(pl.multiple_of(at * chunk, chunk), size * chunk)
        held = taps_held.at[other(unit % others), unit // others, span]
        return remote(held, held, st_send.at[stage, unit], st_recv.at[stage, unit], s, partners[stage])

    units = (sections - 1) * taps
    items = list(range(others)) + [None] + list(range(others, units))

    def arrived(stage, item):
        if item is None:
            if stage < 0:
                for i in range(sections - 1):
                    ly = other(i)
                    remote(slope_own.at[0], slope_z.at[ly], zs_send.at[0], zs_recv.at[ly],
                           s, l).wait_recv()
                slope_all[place] = slope_z[...].reshape(layers * band, channels).astype(bf16)
            else:
                for copy in slope_copies(stage, arrive):
                    copy.wait_recv()
        elif stage < 0:
            ly, t = other(item % others), item // others
            held = taps_held.at[ly, t, mine]
            remote(held, held, zw_send.at[0, 0], zw_recv.at[ly, t], s, l).wait_recv()
        else:
            weight_copy(stage, item, arrive).wait_recv()

    def advance(step):
        for stage in range(3):
            at = step - SKEW * stage
            if 0 <= at < len(items):
                arrived(stage - 1, items[at])
                if items[at] is None:
                    for copy in slope_copies(stage, spans):
                        launch(copy)
                else:
                    launch(weight_copy(stage, items[at], spans))
        at = step - SKEW * 3
        if 0 <= at < len(items):
            arrived(2, items[at])

    def widen():
        for b in range(lons):
            slope_wide[:, b] = slope_all[place_of(b)].astype(f32).reshape(layers, band, channels)

    low = lax.broadcasted_iota(jnp.int32, (lons, pairs, band, channels), 2) < half

    def neighbours(values):
        swapped = pltpu.roll(values.reshape(lons * pairs, band, channels), half, 1)
        swapped = swapped.reshape(lons, pairs, band, channels)
        after = jnp.concatenate([swapped[1:], swapped[:1]], axis=0)
        before = jnp.concatenate([swapped[-1:], swapped[:-1]], axis=0)
        plus = jnp.where(low, swapped, after)
        minus = jnp.where(low, before, swapped)
        return (minus.reshape(rows, channels).astype(bf16), plus.reshape(rows, channels).astype(bf16))

    def forward(n):
        u = field[...].astype(f32)
        minus, plus = neighbours(u)
        conv = jnp.dot(minus, taps_held[n, 0], preferred_element_type=f32)
        conv = conv + jnp.dot(u.astype(bf16), taps_held[n, 1], preferred_element_type=f32)
        conv = conv + jnp.dot(plus, taps_held[n, 2], preferred_element_type=f32)
        slope = slope_wide[n][:, None]
        out = u.reshape(lons, pairs, band, channels) + slope * conv.reshape(lons, pairs, band, channels)
        field[...] = out.reshape(rows, channels).astype(bf16)

    def backward(n):
        c = field[...].astype(f32)
        slope = slope_wide[n][:, None]
        sens = (slope * c.reshape(lons, pairs, band, channels)).reshape(rows, channels).astype(bf16)
        minus, plus = neighbours(sens.astype(f32))
        flip = (((1,), (1,)), ((), ()))
        conv = lax.dot_general(plus, taps_held[n, 0], flip, preferred_element_type=f32)
        conv = conv + lax.dot_general(sens, taps_held[n, 1], flip, preferred_element_type=f32)
        conv = conv + lax.dot_general(minus, taps_held[n, 2], flip, preferred_element_type=f32)
        field[...] = (c + conv).astype(bf16)

    count = lons * pairs
    row_id = lax.broadcasted_iota(jnp.int32, (rows, 128), 0)
    col_id = lax.broadcasted_iota(jnp.int32, (rows, 128), 1)
    vec_of = row_id // band
    onto = [jnp.where(col_id == count * i + vec_of, 1.0, 0.0).astype(f32) for i in range(3)]
    fold = jnp.where(
        lax.broadcasted_iota(jnp.int32, (count, rows), 0)
        == lax.broadcasted_iota(jnp.int32, (count, rows), 1) // band, 1.0, 0.0
    ).astype(f32)
    expand = onto[0][:, :count]
    same = lax.rem(lax.broadcasted_iota(jnp.int32, (rows, rows), 0), band) == lax.rem(
        lax.broadcasted_iota(jnp.int32, (rows, rows), 1), band
    )
    nt = (((1,), (1,)), ((), ()))

    def dot(a, b):
        return jnp.dot(a, b, precision=high, preferred_element_type=f32)

    def dot_nt(a, b):
        return lax.dot_general(a, b, nt, precision=high, preferred_element_type=f32)

    for load in loads[3:]:
        load.wait()
    beta_wide = jnp.where(same, dot_nt(dot(expand, beta_ref[...]), expand), 0.0)
    prev_f = prev_ref[:, 0].astype(f32).reshape(rows, channels)
    resid_ref[...] = dot(beta_wide, prev_f)
    own_bf = block_rows[...].reshape(rows, channels)
    gram_b = lax.dot_general(own_bf, own_bf, nt, preferred_element_type=f32)
    part_b_early = dot(jnp.where(same, gram_b, 0.0), onto[2])

    for step in range(SKEW * 3 + others + 1):
        advance(step)
    widen()
    for d in range(1, lons):
        source = lax.rem(l + d, lons)
        remote(block_rows.at[0], block_in.at[source], in_send.at[0], in_recv.at[source],
               s, l).wait_recv()
    field[...] = block_in[...].reshape(rows, channels)
    own_copy.wait()

    for n in range(sections - 1):
        until = SKEW * 3 + units - others + n + 2
        for step in range(SKEW * 3 + others + 1 if n == 0 else until - 1, until):
            advance(step)
        forward(n)
    forward(sections - 1)
    t4 = field[...].astype(f32).reshape(lons, pairs, band, channels)
    for b in range(lons):
        scale = metric_all[place_of(b)][:, :1]
        field[pl.ds(b * slab, slab)] = (scale[None] * t4[b]).reshape(slab, channels).astype(bf16)
    for n in range(sections - 1, -1, -1):
        backward(n)

    applied_out[...] = field[...].reshape(lons, slab, channels)
    for d in range(1, lons):
        to = lax.rem(l + d, lons)
        launch(remote(applied_out.at[to], applied_in.at[l], out_send.at[d], out_recv.at[l], s, to))
    applied_in[l] = applied_out[l]
    for d in range(1, lons):
        source = lax.rem(l + d, lons)
        remote(applied_out.at[0], applied_in.at[source], out_send.at[0], out_recv.at[source],
               s, l).wait_recv()
    shifted = applied_in[...].reshape(rows, channels).astype(f32) - resid_ref[...]
    own_f = own_bf.astype(f32)
    gram_p = jnp.where(same, dot_nt(own_f, shifted), 0.0)
    gram_s = jnp.where(same, dot_nt(shifted, shifted), 0.0)
    part = dot(fold, dot(gram_p, onto[0]) + dot(gram_s, onto[1]) + part_b_early)

    part_a[l] = part
    for d in range(1, lons):
        to = lax.rem(l + d, lons)
        launch(remote(part_a.at[l], part_a.at[l], pa_send.at[d], pa_recv.at[l], s, to))
    for d in range(1, lons):
        source = lax.rem(l + d, lons)
        remote(part_a.at[source], part_a.at[source], pa_send.at[0], pa_recv.at[source],
               s, l).wait_recv()
    part_b[s] = jnp.sum(part_a[...], axis=0)
    for d in range(1, sections):
        to = lax.rem(s + d, sections)
        launch(remote(part_b.at[s], part_b.at[s], pb_send.at[d], pb_recv.at[s], to, l))
    for d in range(1, sections):
        source = lax.rem(s + d, sections)
        remote(part_b.at[source], part_b.at[source], pb_send.at[0], pb_recv.at[source],
               s, l).wait_recv()
    total = jnp.sum(part_b[...], axis=0) / cells
    projection = total[:, :count]
    shifted_gram = total[:, count : 2 * count]
    block_gram = total[:, 2 * count : 3 * count]
    proj_ref[...] = projection
    tn = (((0,), (0,)), ((), ()))
    bp = dot(block_gram, projection)
    inner = lax.dot_general(
        projection, bp - 2.0 * projection, tn, precision=high, preferred_element_type=f32
    )
    gram_ref[...] = shifted_gram + inner
    proj_wide = jnp.where(same, dot_nt(dot_nt(expand, projection), expand), 0.0)
    resid_ref[...] = shifted - dot(proj_wide, own_f)
    for copy in sends:
        copy.wait_send()


def ring_body(lanczos_block, previous, beta_prev, weights, act_slope, metric):
    f32, bf16 = jnp.float32, jnp.bfloat16
    sections = lax.axis_size("section")
    lons = lax.axis_size("lon")
    count, lat, band, channels = lanczos_block.shape
    pairs = count // lons
    rows = count * band
    slab = pairs * band
    taps = 3
    cells = lat * band * lons * channels
    vmem = pl.BlockSpec(memory_space=pltpu.VMEM)
    dma = pltpu.SemaphoreType.DMA
    units = (sections - 1) * taps
    resid, proj, gram = pl.pallas_call(
        functools.partial(ring_kernel, sections, band, float(cells)),
        out_shape=(
            jax.ShapeDtypeStruct((rows, channels), f32),
            jax.ShapeDtypeStruct((count, count), f32),
            jax.ShapeDtypeStruct((count, count), f32),
        ),
        in_specs=[pl.BlockSpec(memory_space=pl.ANY)] * 6,
        out_specs=(vmem, vmem, vmem),
        scratch_shapes=[
            pltpu.VMEM((sections, taps, channels, channels), bf16),
            pltpu.VMEM((lons, slab, channels), bf16),
            pltpu.VMEM((lons, slab, channels), bf16),
            pltpu.VMEM((lat, band, channels), f32),
            pltpu.VMEM((sections, band, channels), f32),
            pltpu.VMEM((lons, sections * band, channels), bf16),
            pltpu.VMEM((sections, lons, band, channels), f32),
            pltpu.VMEM((lons, band, 128), f32),
            pltpu.VMEM((rows, channels), bf16),
            pltpu.VMEM((lons, slab, channels), bf16),
            pltpu.VMEM((lons, slab, channels), bf16),
            pltpu.VMEM((lons, count, 128), f32),
            pltpu.VMEM((sections, count, 128), f32),
            pltpu.VMEM((count, band, channels), bf16),
            pltpu.VMEM((count, 1, band, channels), bf16),
            pltpu.VMEM((count, count), f32),
            pltpu.VMEM((1, lat, band, channels), bf16),
            pltpu.VMEM((lat, band), f32),
            dma((5,)),
            dma,
            dma((sections,)), dma((sections,)),
            dma((sections, taps)), dma((sections, taps)),
            dma((3,)), dma((3,)), dma((3,)), dma((3,)),
            dma((3, units)), dma((3, units)),
            dma((lons,)), dma((lons,)), dma((lons,)), dma((lons,)),
            dma((lons,)), dma((lons,)), dma((sections,)), dma((sections,)),
        ],
        compiler_params=pltpu.CompilerParams(
            collective_id=0, has_side_effects=True, vmem_limit_bytes=60 * 1024 * 1024
        ),
    )(lanczos_block, previous, beta_prev, weights, act_slope, metric)
    return (resid.reshape(count, previous.shape[1], band, channels), proj, gram)


def step_body(lanczos_block, previous, beta_prev, weights, act_slope, metric):
    count, lat, band, channels = lanczos_block.shape
    lons = lax.axis_size("lon")
    sections = lax.axis_size("section")
    rings = (
        lat <= DILATION_SIZE
        and lat == sections
        and lons == LON_DEVICES
        and band == 2 * DILATION_SIZE
        and count % lons == 0
        and (count // lons * band) % 16 == 0
        and 3 * count <= 128
        and channels % (16 * lons) == 0
    )
    form = ring_body if rings else body
    return form(lanczos_block, previous, beta_prev, weights, act_slope, metric)


def solution(mesh):
    return jax.shard_map(
        step_body,
        mesh=mesh,
        in_specs=(
            P(None, None, "lon", None),
            P(None, "section", "lon", None),
            P(),
            P("section", None, None, None),
            P("section", None, "lon", None),
            P(None, "lon"),
        ),
        out_specs=(P(None, "section", "lon", None), P(), P()),
        check_vma=False,
    )
```

```python
import functools

import jax
import jax.numpy as jnp
from jax import lax
from jax.experimental import pallas as pl
from jax.experimental.pallas import tpu as pltpu
from jax.sharding import PartitionSpec as P

K = 16
DILATION_SIZE = 4
LON_DEVICES = 8
SKEW = 3


def padded(cells, sides, width):
    for axis, dim in sides:
        count = lax.axis_size(axis)
        head = lax.slice_in_dim(cells, 0, width, axis=dim)
        tail = lax.slice_in_dim(cells, cells.shape[dim] - width, cells.shape[dim], axis=dim)
        cells = jnp.concatenate(
            [
                lax.ppermute(tail, axis, [(i, (i + 1) % count) for i in range(count)]),
                cells,
                lax.ppermute(head, axis, [((i + 1) % count, i) for i in range(count)]),
            ],
            axis=dim,
        )
    return cells


def from_behind(shard, axis, by):
    count = lax.axis_size(axis)
    pairs = [(i, i + by) for i in range(count) if 0 <= i + by < count]
    return lax.ppermute(shard, axis, pairs)


def broadcast(shard, axis, root):
    mine = lax.axis_index(axis) == root
    return lax.psum(jnp.where(mine, shard, jnp.zeros_like(shard)), axis)


def spread_taps(input_field, tap_weights, direction_sign, border_width):
    micro_size = input_field.shape[0]
    lat_rows = input_field.shape[1]
    lon_cols = input_field.shape[2] - 2 * border_width
    channels = input_field.shape[3]
    padded_field = jnp.pad(input_field, ((0, 0), (border_width, border_width), (0, 0), (0, 0)))
    summed = jnp.zeros((micro_size * lat_rows * lon_cols, channels), jnp.float32)
    for row_stride in (-1, 0, 1):
        for column_stride in (-1, 0, 1):
            tap_index = 3 * (row_stride + 1) + (column_stride + 1)
            first_row = border_width + direction_sign * row_stride * border_width
            col_start = border_width + direction_sign * column_stride * border_width
            tap_rows = padded_field[
                :, first_row : first_row + lat_rows, col_start : col_start + lon_cols, :
            ].reshape(-1, channels)
            if direction_sign > 0:
                summed = summed + jnp.dot(
                    tap_rows, tap_weights[tap_index], preferred_element_type=jnp.float32
                )
            else:
                summed = summed + lax.dot_general(
                    tap_rows,
                    tap_weights[tap_index],
                    (((1,), (1,)), ((), ())),
                    preferred_element_type=jnp.float32,
                )
    return summed.reshape(micro_size, lat_rows, lon_cols, channels)


def body(lanczos_block, previous, beta_prev, weights, act_slope, metric):
    section_count = lax.axis_size("section")
    section_index = lax.axis_index("section")
    tap_weights = weights[0]
    slope_here = act_slope[0].astype(jnp.float32)[None]
    border_width = DILATION_SIZE
    micro_count = 2
    micro_size = K // micro_count
    slot_shape = (micro_size,) + lanczos_block.shape[1:]
    lon_cols = lanczos_block.shape[2]
    micro_feeds = lanczos_block.reshape((micro_count,) + slot_shape)
    tick_count = micro_count + section_count - 1
    zero_slot = jnp.zeros(slot_shape, jnp.bfloat16)
    empty_store = jnp.zeros((micro_count,) + slot_shape, jnp.bfloat16)

    def forward_layer(rimmed):
        convolved = spread_taps(rimmed, tap_weights, 1, border_width)
        centre = rimmed[:, :, border_width : border_width + lon_cols, :].astype(jnp.float32)
        return (centre + slope_here * convolved).astype(jnp.bfloat16)

    def skip_forward(rimmed):
        return zero_slot

    def forward_tick(state_pair, tick_now):
        inbound, forward_out = state_pair
        micro_index = tick_now - section_index
        active = (micro_index >= 0) & (micro_index < micro_count)
        slot_index = jnp.clip(micro_index, 0, micro_count - 1)
        fed_slot = lax.dynamic_index_in_dim(micro_feeds, slot_index, 0, keepdims=False)
        incoming = jnp.where(section_index == 0, fed_slot, inbound)
        rimmed = padded(incoming, (("lon", 2),), border_width)
        result = lax.cond(active, forward_layer, skip_forward, rimmed)
        keep_slot = active & (section_index == section_count - 1)
        old_slot = lax.dynamic_index_in_dim(forward_out, slot_index, 0, keepdims=False)
        forward_out = lax.dynamic_update_index_in_dim(
            forward_out, jnp.where(keep_slot, result, old_slot), slot_index, 0
        )
        outbound = from_behind(result, "section", 1)
        return ((outbound, forward_out), None)

    (unused_slot, forward_out), unused_out = lax.scan(
        forward_tick, (zero_slot, empty_store), jnp.arange(tick_count, dtype=jnp.int32)
    )
    metric_here = metric[None, :, :, None]

    def backward_layer(operands):
        incoming, rimmed = operands
        convolved = spread_taps(rimmed, tap_weights, -1, border_width)
        return (incoming.astype(jnp.float32) + convolved).astype(jnp.bfloat16)

    def skip_backward(operands):
        return zero_slot

    def backward_tick(state_pair, tick_now):
        inbound, adjoint_out = state_pair
        micro_index = tick_now - (section_count - 1 - section_index)
        active = (micro_index >= 0) & (micro_index < micro_count)
        slot_index = jnp.clip(micro_index, 0, micro_count - 1)
        stored_slot = lax.dynamic_index_in_dim(forward_out, slot_index, 0, keepdims=False)
        started = (metric_here * stored_slot.astype(jnp.float32)).astype(jnp.bfloat16)
        incoming = jnp.where(section_index == section_count - 1, started, inbound)
        sensitivity = (slope_here * incoming.astype(jnp.float32)).astype(jnp.bfloat16)
        rimmed = padded(sensitivity, (("lon", 2),), border_width)
        result = lax.cond(active, backward_layer, skip_backward, (incoming, rimmed))
        keep_slot = active & (section_index == 0)
        old_slot = lax.dynamic_index_in_dim(adjoint_out, slot_index, 0, keepdims=False)
        adjoint_out = lax.dynamic_update_index_in_dim(
            adjoint_out, jnp.where(keep_slot, result, old_slot), slot_index, 0
        )
        outbound = from_behind(result, "section", -1)
        return ((outbound, adjoint_out), None)

    (unused_back, adjoint_out), unused_more = lax.scan(
        backward_tick, (zero_slot, empty_store), jnp.arange(tick_count, dtype=jnp.int32)
    )
    applied = adjoint_out.reshape(lanczos_block.shape)
    applied_all = broadcast(applied, "section", 0)
    row_count = previous.shape[1]
    applied_rows = lax.dynamic_slice_in_dim(applied_all, section_index * row_count, row_count, 1)
    own_block = lax.dynamic_slice_in_dim(lanczos_block, section_index * row_count, row_count, 1)
    high = lax.Precision.HIGHEST
    cell_count = (
        lanczos_block.shape[1]
        * lanczos_block.shape[2]
        * lax.axis_size("lon")
        * lanczos_block.shape[3]
    )
    block_flat = own_block.reshape(K, -1).astype(jnp.float32)
    prev_flat = previous.reshape(K, -1).astype(jnp.float32)
    shifted = applied_rows.reshape(K, -1).astype(jnp.float32) - jnp.dot(
        beta_prev, prev_flat, precision=high
    )
    part_projection = jnp.dot(block_flat, shifted.T, precision=high) / cell_count
    part_shifted = jnp.dot(shifted, shifted.T, precision=high) / cell_count
    part_block = jnp.dot(block_flat, block_flat.T, precision=high) / cell_count
    projection, shifted_gram, block_gram = lax.psum(
        (part_projection, part_shifted, part_block), ("section", "lon")
    )
    residual_rows = shifted - jnp.dot(projection.T, block_flat, precision=high)
    squared_proj = jnp.dot(projection.T, projection, precision=high)
    weighted = jnp.dot(
        projection.T, jnp.dot(block_gram, projection, precision=high), precision=high
    )
    residual_gram = shifted_gram - 2.0 * squared_proj + weighted
    return (residual_rows.reshape(own_block.shape), projection, residual_gram)


def ring_kernel(
    sections, band, cells, block_hbm, prev_hbm, beta_hbm, weights_ref, slope_hbm, metric_hbm,
    resid_ref, proj_ref, gram_ref,
    taps_held, block_rows, block_in, slope_own, slope_z, slope_all, slope_wide, metric_all,
    field, applied_out, applied_in, part_a, part_b,
    block_ref, prev_ref, beta_ref, slope_ref, metric_ref, load_sem,
    own_sem, zs_send, zs_recv, zw_send, zw_recv, sl_send, sl_recv, me_send, me_recv,
    st_send, st_recv, in_send, in_recv, out_send, out_recv, pa_send, pa_recv, pb_send, pb_recv,
):
    f32, bf16 = jnp.float32, jnp.bfloat16
    high = lax.Precision.HIGHEST
    s = lax.axis_index("section")
    l = lax.axis_index("lon")
    lons = LON_DEVICES
    taps = 3
    channels = block_hbm.shape[3]
    pairs = block_hbm.shape[0] // lons
    rows = lons * pairs * band
    slab = pairs * band
    half = band // 2
    layers = sections
    others = sections - 1

    core = lax.rem(l, 2)
    xbit = lax.rem(l // 2, 2)
    ybit = l // 4
    flip_x = l + 2 - 4 * xbit
    flip_y = l + 4 - 8 * ybit
    flip_core = l + 1 - 2 * core
    first = flip_x * (1 - core) + flip_y * core
    second = flip_y * (1 - core) + flip_x * core
    abit = xbit * (1 - core) + ybit * core
    bbit = ybit * (1 - core) + xbit * core
    place = 4 * core + 2 * bbit + abit
    partners = (first, second, flip_core)

    def place_of(device):
        c, x, y = device % 2, (device // 2) % 2, device // 4
        return 4 * c + (2 * y + x if c == 0 else 2 * x + y)

    def remote(src, dst, send, recv, section, lon):
        return pltpu.make_async_remote_copy(
            src_ref=src, dst_ref=dst, send_sem=send, recv_sem=recv,
            device_id=(section, lon), device_id_type=pl.DeviceIdType.MESH,
        )

    def other(i):
        return i + (i - s + layers) // layers

    loads = [
        pltpu.make_async_copy(source, held, load_sem.at[i])
        for i, (source, held) in enumerate((
            (slope_hbm, slope_ref),
            (metric_hbm, metric_ref),
            (block_hbm.at[:, s], block_ref),
            (prev_hbm, prev_ref),
            (beta_hbm, beta_ref),
        ))
    ]
    for load in loads:
        load.start()
    own_copy = pltpu.make_async_copy(weights_ref.at[0, pl.ds(taps, taps)], taps_held.at[s], own_sem)
    own_copy.start()

    barrier = pltpu.get_barrier_semaphore()
    for d in range(1, sections):
        pl.semaphore_signal(
            barrier, inc=1, device_id=(lax.rem(s + d, sections), l),
            device_id_type=pl.DeviceIdType.MESH,
        )
    for d in range(1, lons):
        pl.semaphore_signal(
            barrier, inc=1, device_id=(s, lax.rem(l + d, lons)),
            device_id_type=pl.DeviceIdType.MESH,
        )

    for load in loads[:3]:
        load.wait()
    slope_own[...] = slope_ref[0].astype(f32)
    slope_z[s] = slope_own[s]
    block_f = block_ref[...].astype(f32).reshape(rows, channels)
    block_rows[...] = block_f.astype(bf16).reshape(lons, slab, channels)
    block_in[l] = block_rows[l]
    metric_row = metric_ref[pl.ds(s, 1), :]
    eye = lax.broadcasted_iota(jnp.int32, (band, band), 0) == lax.broadcasted_iota(
        jnp.int32, (band, band), 1
    )
    metric_col = jnp.sum(
        jnp.where(eye, jnp.broadcast_to(metric_row, (band, band)), 0.0), axis=1, keepdims=True
    )
    metric_all[place] = jnp.broadcast_to(metric_col, (band, 128))

    pl.semaphore_wait(barrier, sections - 1 + lons - 1)

    sends = []

    def launch(copy):
        copy.start()
        sends.append(copy)

    chunk = channels // lons
    for d in range(1, sections):
        to = lax.rem(s + d, sections)
        launch(remote(slope_own.at[to], slope_z.at[s], zs_send.at[d], zs_recv.at[s], to, l))
    mine = pl.ds(pl.multiple_of(place * chunk, chunk), chunk)
    for t in range(taps):
        for d in range(sections - 1, 0, -1):
            to = lax.rem(s + d, sections)
            launch(remote(
                weights_ref.at[0, taps + t, mine], taps_held.at[s, t, mine],
                zw_send.at[d, t], zw_recv.at[s, t], to, l,
            ))
    for d in range(1, lons):
        to = lax.rem(l + d, lons)
        launch(remote(block_rows.at[to], block_in.at[l], in_send.at[d], in_recv.at[l], s, to))

    spans = (
        (place, 1),
        (2 * (place // 2), 2),
        (4 * core, 4),
    )
    arrive = (
        (place + 1 - 2 * abit, 1),
        (2 * (place // 2) + 2 - 4 * bbit, 2),
        (4 - 4 * core, 4),
    )

    def slope_copies(stage, where):
        at, size = where[stage]
        span = pl.ds(at, size)
        return (
            remote(slope_all.at[span], slope_all.at[span], sl_send.at[stage], sl_recv.at[stage],
                   s, partners[stage]),
            remote(metric_all.at[span], metric_all.at[span], me_send.at[stage], me_recv.at[stage],
                   s, partners[stage]),
        )

    def weight_copy(stage, unit, where):
        at, size = where[stage]
        span = pl.ds(pl.multiple_of(at * chunk, chunk), size * chunk)
        held = taps_held.at[other(unit % others), unit // others, span]
        return remote(held, held, st_send.at[stage, unit], st_recv.at[stage, unit], s, partners[stage])

    units = (sections - 1) * taps
    items = [None] + list(range(units))

    def arrived(stage, item):
        if item is None:
            if stage < 0:
                for i in range(sections - 1):
                    ly = other(i)
                    remote(slope_own.at[0], slope_z.at[ly], zs_send.at[0], zs_recv.at[ly],
                           s, l).wait_recv()
                slope_all[place] = slope_z[...].reshape(layers * band, channels).astype(bf16)
            else:
                for copy in slope_copies(stage, arrive):
                    copy.wait_recv()
        elif stage < 0:
            ly, t = other(item % others), item // others
            held = taps_held.at[ly, t, mine]
            remote(held, held, zw_send.at[0, 0], zw_recv.at[ly, t], s, l).wait_recv()
        else:
            weight_copy(stage, item, arrive).wait_recv()

    def advance(step):
        for stage in range(3):
            at = step - SKEW * stage
            if 0 <= at < len(items):
                arrived(stage - 1, items[at])
                if items[at] is None:
                    for copy in slope_copies(stage, spans):
                        launch(copy)
                else:
                    launch(weight_copy(stage, items[at], spans))
        at = step - SKEW * 3
        if 0 <= at < len(items):
            arrived(2, items[at])

    def widen():
        for b in range(lons):
            slope_wide[:, b] = slope_all[place_of(b)].astype(f32).reshape(layers, band, channels)

    low = lax.broadcasted_iota(jnp.int32, (lons, pairs, band, channels), 2) < half

    def neighbours(values):
        swapped = pltpu.roll(values.reshape(lons * pairs, band, channels), half, 1)
        swapped = swapped.reshape(lons, pairs, band, channels)
        after = jnp.concatenate([swapped[1:], swapped[:1]], axis=0)
        before = jnp.concatenate([swapped[-1:], swapped[:-1]], axis=0)
        plus = jnp.where(low, swapped, after)
        minus = jnp.where(low, before, swapped)
        return (minus.reshape(rows, channels).astype(bf16), plus.reshape(rows, channels).astype(bf16))

    def forward(n):
        u = field[...].astype(f32)
        minus, plus = neighbours(u)
        conv = jnp.dot(minus, taps_held[n, 0], preferred_element_type=f32)
        conv = conv + jnp.dot(u.astype(bf16), taps_held[n, 1], preferred_element_type=f32)
        conv = conv + jnp.dot(plus, taps_held[n, 2], preferred_element_type=f32)
        slope = slope_wide[n][:, None]
        out = u.reshape(lons, pairs, band, channels) + slope * conv.reshape(lons, pairs, band, channels)
        field[...] = out.reshape(rows, channels).astype(bf16)

    def backward(n):
        c = field[...].astype(f32)
        slope = slope_wide[n][:, None]
        sens = (slope * c.reshape(lons, pairs, band, channels)).reshape(rows, channels).astype(bf16)
        minus, plus = neighbours(sens.astype(f32))
        flip = (((1,), (1,)), ((), ()))
        conv = lax.dot_general(plus, taps_held[n, 0], flip, preferred_element_type=f32)
        conv = conv + lax.dot_general(sens, taps_held[n, 1], flip, preferred_element_type=f32)
        conv = conv + lax.dot_general(minus, taps_held[n, 2], flip, preferred_element_type=f32)
        field[...] = (c + conv).astype(bf16)

    count = lons * pairs
    row_id = lax.broadcasted_iota(jnp.int32, (rows, 128), 0)
    col_id = lax.broadcasted_iota(jnp.int32, (rows, 128), 1)
    vec_of = row_id // band
    onto = [jnp.where(col_id == count * i + vec_of, 1.0, 0.0).astype(f32) for i in range(3)]
    fold = jnp.where(
        lax.broadcasted_iota(jnp.int32, (count, rows), 0)
        == lax.broadcasted_iota(jnp.int32, (count, rows), 1) // band, 1.0, 0.0
    ).astype(f32)
    expand = onto[0][:, :count]
    same = lax.rem(lax.broadcasted_iota(jnp.int32, (rows, rows), 0), band) == lax.rem(
        lax.broadcasted_iota(jnp.int32, (rows, rows), 1), band
    )
    nt = (((1,), (1,)), ((), ()))

    def dot(a, b):
        return jnp.dot(a, b, precision=high, preferred_element_type=f32)

    def dot_nt(a, b):
        return lax.dot_general(a, b, nt, precision=high, preferred_element_type=f32)

    for load in loads[3:]:
        load.wait()
    beta_wide = jnp.where(same, dot_nt(dot(expand, beta_ref[...]), expand), 0.0)
    prev_f = prev_ref[:, 0].astype(f32).reshape(rows, channels)
    resid_ref[...] = dot(beta_wide, prev_f)
    own_bf = block_rows[...].reshape(rows, channels)
    gram_b = lax.dot_general(own_bf, own_bf, nt, preferred_element_type=f32)
    part_b_early = dot(jnp.where(same, gram_b, 0.0), onto[2])

    for step in range(SKEW * 3 + others + 1):
        advance(step)
    widen()
    for d in range(1, lons):
        source = lax.rem(l + d, lons)
        remote(block_rows.at[0], block_in.at[source], in_send.at[0], in_recv.at[source],
               s, l).wait_recv()
    field[...] = block_in[...].reshape(rows, channels)
    own_copy.wait()

    for n in range(sections - 1):
        until = SKEW * 3 + units - others + n + 2
        for step in range(SKEW * 3 + others + 1 if n == 0 else until - 1, until):
            advance(step)
        forward(n)
    forward(sections - 1)
    t4 = field[...].astype(f32).reshape(lons, pairs, band, channels)
    for b in range(lons):
        scale = metric_all[place_of(b)][:, :1]
        field[pl.ds(b * slab, slab)] = (scale[None] * t4[b]).reshape(slab, channels).astype(bf16)
    for n in range(sections - 1, -1, -1):
        backward(n)

    applied_out[...] = field[...].reshape(lons, slab, channels)
    for d in range(1, lons):
        to = lax.rem(l + d, lons)
        launch(remote(applied_out.at[to], applied_in.at[l], out_send.at[d], out_recv.at[l], s, to))
    applied_in[l] = applied_out[l]
    for d in range(1, lons):
        source = lax.rem(l + d, lons)
        remote(applied_out.at[0], applied_in.at[source], out_send.at[0], out_recv.at[source],
               s, l).wait_recv()
    shifted = applied_in[...].reshape(rows, channels).astype(f32) - resid_ref[...]
    own_f = own_bf.astype(f32)
    gram_p = jnp.where(same, dot_nt(own_f, shifted), 0.0)
    gram_s = jnp.where(same, dot_nt(shifted, shifted), 0.0)
    part = dot(fold, dot(gram_p, onto[0]) + dot(gram_s, onto[1]) + part_b_early)

    part_a[l] = part
    for d in range(1, lons):
        to = lax.rem(l + d, lons)
        launch(remote(part_a.at[l], part_a.at[l], pa_send.at[d], pa_recv.at[l], s, to))
    for d in range(1, lons):
        source = lax.rem(l + d, lons)
        remote(part_a.at[source], part_a.at[source], pa_send.at[0], pa_recv.at[source],
               s, l).wait_recv()
    part_b[s] = jnp.sum(part_a[...], axis=0)
    for d in range(1, sections):
        to = lax.rem(s + d, sections)
        launch(remote(part_b.at[s], part_b.at[s], pb_send.at[d], pb_recv.at[s], to, l))
    for d in range(1, sections):
        source = lax.rem(s + d, sections)
        remote(part_b.at[source], part_b.at[source], pb_send.at[0], pb_recv.at[source],
               s, l).wait_recv()
    total = jnp.sum(part_b[...], axis=0) / cells
    projection = total[:, :count]
    shifted_gram = total[:, count : 2 * count]
    block_gram = total[:, 2 * count : 3 * count]
    proj_ref[...] = projection
    tn = (((0,), (0,)), ((), ()))
    bp = dot(block_gram, projection)
    inner = lax.dot_general(
        projection, bp - 2.0 * projection, tn, precision=high, preferred_element_type=f32
    )
    gram_ref[...] = shifted_gram + inner
    proj_wide = jnp.where(same, dot_nt(dot_nt(expand, projection), expand), 0.0)
    resid_ref[...] = shifted - dot(proj_wide, own_f)
    for copy in sends:
        copy.wait_send()


def ring_body(lanczos_block, previous, beta_prev, weights, act_slope, metric):
    f32, bf16 = jnp.float32, jnp.bfloat16
    sections = lax.axis_size("section")
    lons = lax.axis_size("lon")
    count, lat, band, channels = lanczos_block.shape
    pairs = count // lons
    rows = count * band
    slab = pairs * band
    taps = 3
    cells = lat * band * lons * channels
    vmem = pl.BlockSpec(memory_space=pltpu.VMEM)
    dma = pltpu.SemaphoreType.DMA
    units = (sections - 1) * taps
    resid, proj, gram = pl.pallas_call(
        functools.partial(ring_kernel, sections, band, float(cells)),
        out_shape=(
            jax.ShapeDtypeStruct((rows, channels), f32),
            jax.ShapeDtypeStruct((count, count), f32),
            jax.ShapeDtypeStruct((count, count), f32),
        ),
        in_specs=[pl.BlockSpec(memory_space=pl.ANY)] * 6,
        out_specs=(vmem, vmem, vmem),
        scratch_shapes=[
            pltpu.VMEM((sections, taps, channels, channels), bf16),
            pltpu.VMEM((lons, slab, channels), bf16),
            pltpu.VMEM((lons, slab, channels), bf16),
            pltpu.VMEM((lat, band, channels), f32),
            pltpu.VMEM((sections, band, channels), f32),
            pltpu.VMEM((lons, sections * band, channels), bf16),
            pltpu.VMEM((sections, lons, band, channels), f32),
            pltpu.VMEM((lons, band, 128), f32),
            pltpu.VMEM((rows, channels), bf16),
            pltpu.VMEM((lons, slab, channels), bf16),
            pltpu.VMEM((lons, slab, channels), bf16),
            pltpu.VMEM((lons, count, 128), f32),
            pltpu.VMEM((sections, count, 128), f32),
            pltpu.VMEM((count, band, channels), bf16),
            pltpu.VMEM((count, 1, band, channels), bf16),
            pltpu.VMEM((count, count), f32),
            pltpu.VMEM((1, lat, band, channels), bf16),
            pltpu.VMEM((lat, band), f32),
            dma((5,)),
            dma,
            dma((sections,)), dma((sections,)),
            dma((sections, taps)), dma((sections, taps)),
            dma((3,)), dma((3,)), dma((3,)), dma((3,)),
            dma((3, units)), dma((3, units)),
            dma((lons,)), dma((lons,)), dma((lons,)), dma((lons,)),
            dma((lons,)), dma((lons,)), dma((sections,)), dma((sections,)),
        ],
        compiler_params=pltpu.CompilerParams(
            collective_id=0, has_side_effects=True, vmem_limit_bytes=60 * 1024 * 1024
        ),
    )(lanczos_block, previous, beta_prev, weights, act_slope, metric)
    return (resid.reshape(count, previous.shape[1], band, channels), proj, gram)


def step_body(lanczos_block, previous, beta_prev, weights, act_slope, metric):
    count, lat, band, channels = lanczos_block.shape
    lons = lax.axis_size("lon")
    sections = lax.axis_size("section")
    rings = (
        lat <= DILATION_SIZE
        and lat == sections
        and lons == LON_DEVICES
        and band == 2 * DILATION_SIZE
        and count % lons == 0
        and (count // lons * band) % 16 == 0
        and 3 * count <= 128
        and channels % (16 * lons) == 0
    )
    form = ring_body if rings else body
    return form(lanczos_block, previous, beta_prev, weights, act_slope, metric)


def solution(mesh):
    return jax.shard_map(
        step_body,
        mesh=mesh,
        in_specs=(
            P(None, None, "lon", None),
            P(None, "section", "lon", None),
            P(),
            P("section", None, None, None),
            P("section", None, "lon", None),
            P(None, "lon"),
        ),
        out_specs=(P(None, "section", "lon", None), P(), P()),
        check_vma=False,
    )
```
